32 devices in a mesh: row: 8 (over z, x), col: 4 (over y, core).
Axes of the slice: x: 2, y: 2, z: 4, core: 2. Of those that a mesh axis runs over, the one named last changes fastest.
Arguments:
- hidden: bfloat16 [2560, 8192], P('row', 'col'), may hold values from -6 to 6
- w_query: bfloat16 [8192, 8192], P('col', 'row'), may hold values from -0.0625 to 0.0625
- w_keyval: bfloat16 [8192, 2048], P('col', 'row'), may hold values from -0.15625 to 0.15625
- prefix_cache: bfloat16 [2, 16384, 2048], P(None, 'col', 'row'), may hold values from -60 to 60, as said below
- suffix_lengths: int32 [16], replicated, may hold values from 32 to 160, as said below
- group_ids: int32 [16], replicated, may hold values from 0 to 1, as said below
Outputs:
- attended: bfloat16 [2560, 8192], P('col', 'row')
The draws below stay inside these ranges and needn't reach their ends.
Inputs may be any that keep to these rules, and one draw needn't show every extreme that they name: `suffix_lengths`: every suffix has 32 to 160 live tokens; some request has exactly 160 and some exactly 32. `group_ids`: exactly 8 requests read each prefix. `prefix_cache`: finite values.
All inputs are finite; a program needn't handle non-finite values.
Results may differ from the reference program's by a relative error of at most 0.011.
Values may be sent and summed in bfloat16 or wider, within the bound.
A program may use at most 128 MiB of HBM per device.

```python
import jax
import jax.numpy as jnp
from jax import lax

D = 8192
HQ = 64
KVH = 8
HD = 128
PREFIX = 16384
SUF = 160
MIN_SUF = 32
GROUPS = 2
REQ_G = 8
REQ = 16
TOK = 2560


def draw_suffix_lengths(key, part):
    values = jax.random.randint(jax.random.fold_in(key, 3), (REQ,), MIN_SUF, SUF + 1)
    order = jax.random.permutation(jax.random.fold_in(key, 11), REQ)
    values = jnp.where(order == 0, SUF, jnp.where(order == 1, MIN_SUF, values))
    return values.astype(jnp.int32)


def draw_group_ids(key, part):
    order = jax.random.permutation(jax.random.fold_in(key, 5), REQ)
    return (order >= REQ_G).astype(jnp.int32)


def draw_prefix_cache(key, part):
    width = 2 * KVH * HD
    base = 2.5 * jax.random.normal(jax.random.fold_in(key, 7), (GROUPS, PREFIX, width), jnp.float32)
    base = jnp.clip(base, -15.0, 15.0)
    return base.astype(jnp.bfloat16)


def block_levels(key, extent, pieces, smallest, top_value):
    gain = 1.0
    for dim, parts in pieces:
        heights = jax.random.uniform(jax.random.fold_in(jax.random.fold_in(key, 6), dim), (parts,), jnp.float32, smallest / len(pieces), top_value / len(pieces))
        gain = gain * jnp.repeat(jnp.exp(heights), extent[dim] // parts).reshape((-1,) + (1,) * (len(extent) - 1 - dim))
    return gain


def gaussian(own_key, extent, spread, limit, pieces=(), kind=jnp.bfloat16):
    gain = block_levels(own_key, extent, pieces, -0.22, 0.18) if pieces else 1.0
    entries = jax.random.normal(own_key, extent, jnp.float32) * spread * gain
    return jnp.minimum(jnp.maximum(entries, -limit), limit).astype(kind)


def setup_inputs(seed: int = 0) -> dict:
    key_of = jax.random.split(jax.random.key(seed), 7)
    return {
        "hidden": gaussian(key_of[0], (TOK, D), 1.0, 6.0, ((0, 8), (1, 4))),
        "w_query": gaussian(key_of[1], (D, HQ * HD), D ** -0.5, 0.0625, ((0, 4), (1, 8))),
        "w_keyval": gaussian(key_of[2], (D, 2 * KVH * HD), (D // 6) ** -0.5, 0.15625, ((0, 4), (1, 8))),
        "prefix_cache": draw_prefix_cache(jax.random.fold_in(key_of[6], 71), 0),
        "suffix_lengths": draw_suffix_lengths(jax.random.fold_in(key_of[6], 71), 0),
        "group_ids": draw_group_ids(jax.random.fold_in(key_of[6], 71), 0),
    }


def rotary_tables(positions):
    freqs = 500000.0 ** (-(jnp.arange(HD // 2, dtype=jnp.float32) * 2.0 / HD))
    angles = positions.astype(jnp.float32)[:, None] * freqs[None, :]
    return jnp.cos(angles), jnp.sin(angles)


def rotate(values, cosine, sine):
    first = values[..., : HD // 2]
    second = values[..., HD // 2:]
    cosine = cosine[:, None, :]
    sine = sine[:, None, :]
    return jnp.concatenate([first * cosine - second * sine, second * cosine + first * sine], axis=-1)


def reference(hidden, w_query, w_keyval, prefix_cache, suffix_lengths, group_ids):
    slots = hidden.shape[0]
    positions = PREFIX + jnp.arange(slots, dtype=jnp.int32) % SUF
    cosine, sine = rotary_tables(positions)
    query = jnp.dot(hidden, w_query, preferred_element_type=jnp.float32).reshape(slots, HQ, HD)
    query = rotate(query, cosine, sine).astype(jnp.bfloat16)
    keyval = jnp.dot(hidden, w_keyval, preferred_element_type=jnp.float32).reshape(slots, KVH, 2, HD)
    suffix_keys = rotate(keyval[:, :, 0], cosine, sine).astype(jnp.bfloat16)
    suffix_values = keyval[:, :, 1].astype(jnp.bfloat16)
    cache = prefix_cache.reshape(GROUPS, PREFIX, KVH, 2, HD)
    group_size = HQ // KVH
    query = query.reshape(REQ, SUF, KVH, group_size, HD)
    suffix_keys = suffix_keys.reshape(REQ, SUF, KVH, HD)
    suffix_values = suffix_values.reshape(REQ, SUF, KVH, HD)
    scale = 1.0 / (HD ** 0.5)

    def per_request(inputs_one):
        req_query, req_keys, req_values, group, length = inputs_one
        chosen = lax.dynamic_index_in_dim(cache, group, 0, keepdims=False)
        places = jnp.arange(SUF, dtype=jnp.int32)
        own_mask = (places[None, :] <= places[:, None]) & (places[None, :] < length)
        full_mask = jnp.concatenate([jnp.ones((SUF, PREFIX), dtype=bool), own_mask], axis=1)

        def per_head(head):
            head_query = lax.dynamic_index_in_dim(req_query, head, 1, keepdims=False)
            head_cache = lax.dynamic_index_in_dim(chosen, head, 1, keepdims=False)
            all_keys = jnp.concatenate([head_cache[:, 0], lax.dynamic_index_in_dim(req_keys, head, 1, keepdims=False)], axis=0)
            all_values = jnp.concatenate([head_cache[:, 1], lax.dynamic_index_in_dim(req_values, head, 1, keepdims=False)], axis=0)
            scores = jnp.einsum("tgd,kd->gtk", head_query.astype(jnp.float32), all_keys.astype(jnp.float32)) * scale
            scores = jnp.where(full_mask[None], scores, -1e30)
            top = jnp.max(scores, axis=-1, keepdims=True)
            weights = jnp.exp(scores - top)
            total = jnp.sum(weights, axis=-1)
            rounded = lax.optimization_barrier(weights.astype(jnp.bfloat16))
            accum = jnp.einsum("gtk,kd->gtd", rounded.astype(jnp.float32), all_values.astype(jnp.float32))
            return accum / total[..., None]

        result = lax.map(per_head, jnp.arange(KVH, dtype=jnp.int32))
        result = jnp.transpose(result, (2, 0, 1, 3))
        live = (places < length).astype(jnp.float32)
        result = result * live[:, None, None, None]
        return result.reshape(SUF, HQ * HD)

    output = lax.map(per_request, (query, suffix_keys, suffix_values, group_ids, suffix_lengths))
    return output.reshape(slots, HQ * HD).astype(jnp.bfloat16)
```

```python
import functools
import math

import jax
import jax.numpy as jnp
from jax import lax
from jax.experimental import pallas as pl
from jax.experimental.pallas import tpu as pltpu
from jax.sharding import PartitionSpec as P

HD = 128
PREFIX = 16384
SUF = 160
SUF_PAD = 256
MASKED = -1e30


def swap(value, axis, mask):
    pairs = [(source, source ^ mask) for source in range(lax.axis_size(axis))]
    return lax.ppermute(value, axis, pairs)


def shift(value, axis, step):
    size = lax.axis_size(axis)
    return lax.ppermute(value, axis, [(source, (source + step) % size) for source in range(size)])


def rotary_tables(positions):
    freqs = 500000.0 ** (-(jnp.arange(HD // 2, dtype=jnp.float32) * 2.0 / HD))
    angles = positions.astype(jnp.float32)[:, None] * freqs[None, :]
    return (jnp.cos(angles), jnp.sin(angles))


def rotate(values, cosine, sine):
    first = values[..., : HD // 2]
    second = values[..., HD // 2 :]
    cosine = cosine[:, None, :]
    sine = sine[:, None, :]
    return jnp.concatenate(
        [first * cosine - second * sine, second * cosine + first * sine], axis=-1
    )


def scores_of(query, keys):
    return lax.dot_general(
        query, keys, (((1,), (1,)), ((), ())), preferred_element_type=jnp.float32
    )


def attend_kernel(n_pieces, tile, pair, groups, lengths, q_ref, own_ref, *refs):
    pieces = refs[:n_pieces]
    out_ref, accum_ref, top_ref, values_ref = refs[n_pieces:]
    request, block, n_blocks = pl.program_id(0), pl.program_id(1), pl.num_programs(1)
    length = lengths[request]
    block_keys = pieces[0].shape[1]
    rows = pair * SUF
    n_pairs = q_ref.shape[1] // (pair * HD)

    @pl.when((request == 0) & (block == 0))
    def _():
        values_ref[:, :, HD:] = jnp.ones((n_pieces, block_keys, HD), jnp.bfloat16)

    for place in range(n_pieces):
        values_ref[place, :, :HD] = pieces[place][0, :, HD:]

    def places(columns):
        row = lax.broadcasted_iota(jnp.int32, (SUF, columns), 0)
        return jnp.concatenate([row] * pair, axis=0)

    def per_pair(index, carry):
        here = pl.ds(pl.multiple_of(index * rows, 32), rows)
        query = jnp.concatenate(
            [
                q_ref[:, pl.ds(pl.multiple_of((index * pair + head) * HD, HD), HD)]
                for head in range(pair)
            ],
            axis=0,
        )

        @pl.when(block == 0)
        def _():
            scores = scores_of(query, own_ref[:, :HD])
            column = lax.broadcasted_iota(jnp.int32, (rows, SUF_PAD), 1)
            mask = (column <= places(SUF_PAD)) & (column < length)
            scores = jnp.where(mask, scores, MASKED)
            top = jnp.max(scores, axis=1, keepdims=True)
            weights = jnp.where(mask, jnp.exp2(scores - top), 0.0).astype(jnp.bfloat16)
            own_values = jnp.concatenate(
                [own_ref[:, HD:], jnp.ones((SUF_PAD, HD), jnp.bfloat16)], axis=1
            )
            accum_ref[here, :] = jnp.dot(weights, own_values, preferred_element_type=jnp.float32)
            top_ref[here, :] = jnp.broadcast_to(top, (rows, HD))

        accum = accum_ref[here, :]
        top = top_ref[here, :1]
        spots = [(place, at) for place in range(n_pieces) for at in range(0, block_keys, tile)]

        def score_tile(spot):
            return scores_of(query, pieces[spot[0]][0, spot[1] : spot[1] + tile, :HD])

        ahead = score_tile(spots[0])
        for number, (place, at) in enumerate(spots):
            scores = ahead
            if number + 1 < len(spots):
                ahead = score_tile(spots[number + 1])
            new_top = jnp.maximum(top, jnp.max(scores, axis=1, keepdims=True))
            weights = jnp.exp2(scores - new_top).astype(jnp.bfloat16)
            accum = accum * jnp.exp2(top - new_top) + jnp.dot(
                weights, values_ref[place, at : at + tile, :], preferred_element_type=jnp.float32
            )
            top = new_top
        accum_ref[here, :] = accum
        top_ref[here, :] = jnp.broadcast_to(top, (rows, HD))

        @pl.when(block == n_blocks - 1)
        def _():
            result = accum[:, :HD] / accum[:, HD:]
            result = jnp.where(places(HD) < length, result, 0.0).astype(out_ref.dtype)
            for head in range(pair):
                out_ref[:, pl.ds(pl.multiple_of((index * pair + head) * HD, HD), HD)] = result[
                    head * SUF : (head + 1) * SUF
                ]

        return carry

    lax.fori_loop(0, n_pairs, per_pair, 0)


def attend(query, own, pieces, groups, lengths):
    n_requests = query.shape[0] // SUF
    width = query.shape[1]
    n_pieces = len(pieces)
    block_keys = min(2048, pieces[0].shape[1])
    n_blocks = pieces[0].shape[1] // block_keys
    tile = min(2048, block_keys)
    pair = 2
    heads = width // HD
    keys = PREFIX + SUF
    flops = 4 * n_requests * SUF * heads * keys * HD
    grid_spec = pltpu.PrefetchScalarGridSpec(
        num_scalar_prefetch=2,
        grid=(n_requests, n_blocks),
        in_specs=[
            pl.BlockSpec((SUF, width), lambda i, j, g, n: (i, 0)),
            pl.BlockSpec((SUF_PAD, 2 * HD), lambda i, j, g, n: (i, 0)),
        ]
        + [pl.BlockSpec((1, block_keys, 2 * HD), lambda i, j, g, n: (g[i], j, 0))] * n_pieces,
        out_specs=pl.BlockSpec((SUF, width), lambda i, j, g, n: (i, 0)),
        scratch_shapes=[
            pltpu.VMEM((heads * SUF, 2 * HD), jnp.float32),
            pltpu.VMEM((heads * SUF, HD), jnp.float32),
            pltpu.VMEM((n_pieces, block_keys, 2 * HD), jnp.bfloat16),
        ],
    )
    return pl.pallas_call(
        functools.partial(attend_kernel, n_pieces, tile, pair),
        grid_spec=grid_spec,
        out_shape=jax.ShapeDtypeStruct(query.shape, jnp.bfloat16),
        compiler_params=pltpu.CompilerParams(
            dimension_semantics=("arbitrary", "arbitrary"), vmem_limit_bytes=56 * 2**20
        ),
        cost_estimate=pl.CostEstimate(
            flops=2 * flops,
            bytes_accessed=n_requests * keys * 4 * HD,
            transcendentals=n_requests * SUF * heads * keys,
        ),
        name="attend",
    )(groups, lengths, query, own, *pieces)


def per_device(hidden, w_query, w_keyval, prefix_cache, suffix_lengths, group_ids):
    n_row = lax.axis_size("row")
    n_col = lax.axis_size("col")
    row_id = lax.axis_index("row")
    col_id = lax.axis_index("col")
    heads_here = w_query.shape[1] // HD
    segments = w_keyval.shape[1] // HD
    n_chunks = hidden.shape[0] // SUF
    shards_per_col = n_row // n_col
    col_tokens = shards_per_col * SUF
    col_bits = n_col.bit_length() - 1

    cache = prefix_cache
    if segments == 1:
        other = swap(cache, "row", 1)
        is_even = row_id % 2 == 0
        cache = jnp.concatenate(
            [jnp.where(is_even, cache, other), jnp.where(is_even, other, cache)], axis=-1
        )
    pieces = [cache]
    for bit in reversed(range(col_bits)):
        pieces = pieces + [swap(piece, "col", 2**bit) for piece in pieces]

    weights_all = jnp.concatenate([w_query, w_keyval], axis=1)
    width = weights_all.shape[1]
    positions = PREFIX + jnp.arange(col_tokens, dtype=jnp.int32) % SUF
    cosine, sine = rotary_tables(positions)
    factor = math.log2(math.e) / HD**0.5
    lengths_all = suffix_lengths.reshape(n_col, shards_per_col, n_chunks)
    groups_all = group_ids.reshape(n_col, shards_per_col, n_chunks)
    lengths_here = lax.dynamic_index_in_dim(lengths_all, col_id, 0, keepdims=False)
    groups_here = lax.dynamic_index_in_dim(groups_all, col_id, 0, keepdims=False)

    outputs = []
    for chunk in range(n_chunks):
        block = hidden[chunk * SUF : (chunk + 1) * SUF]
        gathered = jnp.zeros((n_row,) + block.shape, block.dtype)
        for step in range(n_row // 2):
            if step:
                block = shift(block, "row", 2)
            other = swap(block, "row", 1)
            source = (row_id - 2 * step) % n_row
            gathered = lax.dynamic_update_index_in_dim(gathered, block, source, 0)
            gathered = lax.dynamic_update_index_in_dim(gathered, other, source ^ 1, 0)
        partial = jnp.dot(
            gathered.reshape(n_row * SUF, -1), weights_all, preferred_element_type=jnp.float32
        )

        partial = partial.reshape(n_col, col_tokens, width)
        for bit in range(col_bits):
            mine = (col_id // 2**bit) % 2
            halves = partial.reshape(partial.shape[0] // 2, 2, col_tokens, width)
            kept = lax.dynamic_index_in_dim(halves, mine, 1, keepdims=False)
            given = lax.dynamic_index_in_dim(halves, 1 - mine, 1, keepdims=False)
            if bit:
                given = given.astype(jnp.bfloat16)
            partial = kept + swap(given, "col", 2**bit).astype(jnp.float32)
        projected = partial.reshape(col_tokens, width)

        query = projected[:, : heads_here * HD].reshape(col_tokens, heads_here, HD)
        query = (rotate(query, cosine, sine) * factor).astype(jnp.bfloat16)
        query = query.reshape(col_tokens, heads_here * HD)
        keyval = projected[:, heads_here * HD :].reshape(col_tokens, segments, HD)
        segment_ids = row_id * segments + jnp.arange(segments, dtype=jnp.int32)
        is_key = segment_ids % 2 == 0
        keyval = jnp.where(is_key[None, :, None], rotate(keyval, cosine, sine), keyval)
        keyval = keyval.astype(jnp.bfloat16).reshape(col_tokens, segments * HD)
        if segments == 1:
            other = swap(keyval, "row", 1)
            is_even = row_id % 2 == 0
            keyval = jnp.concatenate(
                [jnp.where(is_even, keyval, other), jnp.where(is_even, other, keyval)], axis=-1
            )
        own = keyval.reshape(shards_per_col, SUF, 2 * HD)
        own = jnp.pad(own, ((0, 0), (0, SUF_PAD - SUF), (0, 0)))
        own = own.reshape(shards_per_col * SUF_PAD, 2 * HD)
        outputs.append(
            attend(query, own, pieces, groups_here[:, chunk], lengths_here[:, chunk])
        )
    if n_chunks == 1:
        return outputs[0]
    parts = [one.reshape(shards_per_col, 1, SUF, heads_here * HD) for one in outputs]
    return jnp.concatenate(parts, axis=1).reshape(-1, heads_here * HD)


def solution(mesh):
    return jax.shard_map(
        per_device,
        mesh=mesh,
        in_specs=(
            P("row", "col"),
            P("col", "row"),
            P("col", "row"),
            P(None, "col", "row"),
            P(),
            P(),
        ),
        out_specs=P("col", "row"),
        check_vma=False,
    )
```
